32 devices in a mesh: groups: 2 (over y), space: 16 (over z, x, core).
Axes of the slice: x: 2, y: 2, z: 4, core: 2. Of those that a mesh axis runs over, the one named last changes fastest.
Arguments:
- actions: float32 [32, 8, 16, 2, 128], P(('groups', 'space')), parts along dimension 0, may hold values from -160 to 160
Outputs:
- q_fields: float32 [32, 8, 16, 2, 128], P(('groups', 'space')), parts along dimension 0
- r_factor: float32 [128, 64], P('groups'), parts along dimension 0
- first_factor: float32 [128, 64], P('groups'), parts along dimension 0
The draws below stay inside these ranges and needn't reach their ends.
There are 2 independent parts, one for each index of `groups`. The reference program is written for one: setup_inputs(seed, part) draws one part's arguments, and reference() takes and returns one part's arrays. A program takes and returns all parts, laid end to end along the dimension named above; each array names one. Nothing has to cross between parts.
All inputs are finite; a program needn't handle non-finite values.
Results may differ from the reference program's by a relative error of at most 0.0003.
Values sent between devices are 32-bit elements; how exact they have to be, the bound alone decides.
A program may use at most 64 MiB of HBM per device.

```python
import math
import jax
import jax.numpy as jnp
from jax import lax

K = 64
KG = 8
SWEEPS = 3
YS = 2
NZ = 128
SLABS = 2
NX = 16
NY = 4


def draw_actions(key, part):
    key = jax.random.fold_in(key, 7)
    key_own, key_common, key_weight, key_scale = jax.random.split(key, 4)
    group_count = K // KG
    shape = (group_count, SLABS, KG, NX, YS, NZ)
    common_shape = (3, 1, SLABS, 1, NX, YS, NZ)
    weight_shape = (3, group_count, 1, KG, 1, 1, 1)
    along_x = jnp.arange(NX, dtype=jnp.float32).reshape(1, 1, 1, NX, 1, 1) / NX
    own = jnp.clip(jax.random.normal(key_own, shape, jnp.float32), -5.0, 5.0)
    commons = jnp.clip(jax.random.normal(key_common, common_shape, jnp.float32), -4.0, 4.0)
    weights = jnp.clip(jax.random.normal(key_weight, weight_shape, jnp.float32), -2.5, 2.5)
    share = 0.025
    spread = jnp.exp(jax.random.uniform(key_scale, (group_count, 1, KG, 1, 1, 1), jnp.float32, math.log(0.3), math.log(3.0)))
    envelope = jnp.exp(1.0986 * along_x)
    mixed = weights[0] * commons[0] + weights[1] * commons[1] + weights[2] * commons[2]
    mixed = mixed * (1.0 / math.sqrt(3.0))
    values = spread * envelope * (mixed + share * own)
    values = values.transpose(1, 0, 2, 3, 4, 5)
    return values.reshape(SLABS * group_count, KG, NX, YS, NZ)


def setup_inputs(seed: int = 0, part: int = 0) -> dict:
    seeds = jax.random.split(jax.random.key(seed), 2)
    own_keys = jax.random.split(jax.random.fold_in(seeds[1], part), 2)
    actions = draw_actions(jax.random.fold_in(jax.random.fold_in(seeds[1], part), 71), part)
    return dict(actions=actions)


damping = 1.0 / 7.0
highest = lax.Precision.HIGHEST

def neighbours(padded):
    total = padded[..., 2:, 1:-1, 1:-1] + padded[..., :-2, 1:-1, 1:-1]
    total = total + padded[..., 1:-1, 2:, 1:-1] + padded[..., 1:-1, :-2, 1:-1]
    total = total + padded[..., 1:-1, 1:-1, 2:] + padded[..., 1:-1, 1:-1, :-2]
    return total

def factor(gram):
    factor_low = jnp.linalg.cholesky(gram)
    identity = jnp.eye(gram.shape[0], dtype=gram.dtype)
    inverse = lax.linalg.triangular_solve(factor_low, identity, left_side=True, lower=True)
    return (factor_low, inverse)

def smooth_one(source):
    smoothed = source * damping
    for sweep_index in range(SWEEPS):
        smoothed = (source + neighbours(jnp.pad(smoothed, 1))) * damping
    return smoothed

def reference(actions):
    group_count = K // KG
    arranged = actions.reshape(SLABS, group_count, KG, NX, YS, NZ).transpose(1, 2, 3, 0, 4, 5)
    fields = arranged.reshape(K, NX, NY, NZ)
    smoothed = lax.map(smooth_one, fields)
    matrix = smoothed.reshape(K, NX * NY * NZ)
    gram_one = jnp.dot(matrix.astype(jnp.float32), matrix.T.astype(jnp.float32), precision=highest, preferred_element_type=jnp.float32)
    low_one, inverse_one = factor(gram_one)
    basis_one = jnp.dot(inverse_one.astype(jnp.float32), matrix.astype(jnp.float32), precision=highest, preferred_element_type=jnp.float32)
    gram_two = jnp.dot(basis_one.astype(jnp.float32), basis_one.T.astype(jnp.float32), precision=highest, preferred_element_type=jnp.float32)
    low_two, inverse_two = factor(gram_two)
    basis = jnp.dot(inverse_two.astype(jnp.float32), basis_one.astype(jnp.float32), precision=highest, preferred_element_type=jnp.float32)
    scale = math.sqrt(NX * NY * NZ)
    scaled = (basis * scale).reshape(group_count, KG, NX, SLABS, YS, NZ).transpose(3, 0, 1, 2, 4, 5)
    q_fields = scaled.reshape(SLABS * group_count, KG, NX, YS, NZ)
    r_factor = jnp.dot(low_one.astype(jnp.float32), low_two.astype(jnp.float32), precision=highest, preferred_element_type=jnp.float32).T / scale
    first_factor = low_one.T / scale
    return (q_fields, r_factor, first_factor)
```

```python
import functools
import math

import jax
import jax.numpy as jnp
from jax import lax
from jax.experimental import pallas as pl
from jax.experimental.pallas import tpu as pltpu
from jax.sharding import PartitionSpec as P

K = 64
YS = 2
highest = lax.Precision.HIGHEST
MESH = pl.DeviceIdType.MESH


def slab_offsets(slabs):
    return sorted({d % slabs for d in (1, -1, 2, -2)} - {0})


def walks(p, q, rows):
    gap = jnp.abs(p - q)
    low, high = jnp.minimum(p, q), jnp.maximum(p, q)
    at_start = jnp.where(low == 0, 1, 0)
    at_end = jnp.where(high == rows - 1, 1, 0)
    one = jnp.where(gap == 1, 1, 0)
    two = jnp.where(gap == 2, 1, 0) + jnp.where(gap == 0, 2 - at_start - at_end, 0)
    three = jnp.where(gap == 3, 1, 0) + jnp.where(gap == 1, 3 - at_start - at_end, 0)
    return one.astype(jnp.float32), two.astype(jnp.float32), three.astype(jnp.float32)


def eliminate(gram):
    lane = lax.broadcasted_iota(jnp.int32, (K, 128), 1)
    row_id = lax.broadcasted_iota(jnp.int32, (K, 128), 0)
    full = jnp.where(lane < K, gram, jnp.where(lane - K == row_id, 1.0, 0.0))
    blocks = [full[8 * i : 8 * i + 8] for i in range(K // 8)]
    sub = lax.broadcasted_iota(jnp.int32, (8, 128), 0)
    count = len(blocks)
    shape = (8, 128)
    scaled = []
    for t in range(count):
        cols = [
            {i: jnp.broadcast_to(blocks[i][:, 8 * t + k : 8 * t + k + 1], shape) for i in range(t, count)}
            for k in range(8)
        ]
        pivots = jnp.ones(shape, jnp.float32)
        for r in range(8):
            pivot = jnp.broadcast_to(cols[r][t][r : r + 1], shape)
            pivots = jnp.where(sub == r, pivot, pivots)
            inverse = 1.0 / pivot
            factors = {i: cols[r][i] * inverse for i in range(t, count)}
            factors[t] = jnp.where(sub > r, factors[t], 0.0)
            for k in range(r + 1, 8):
                value = jnp.broadcast_to(cols[r][t][k : k + 1], shape)
                for i in range(t, count):
                    cols[k][i] = cols[k][i] - factors[i] * value
            row = jnp.broadcast_to(blocks[t][r : r + 1], shape)
            for i in range(t, count):
                blocks[i] = blocks[i] - factors[i] * row
        scaled.append(blocks[t] * lax.rsqrt(pivots))
    done = jnp.concatenate(scaled, axis=0)
    offset = jnp.where(lane < K, lane - row_id, row_id + K - lane)
    return jnp.where(offset >= 0, done, 0.0)


def kernel(
    slabs, groups, scale,
    fields, q_out, r_out, first_out,
    own_send, cross_send, own_recv, cross_recv, rs_send, rs_recv, ag_send, ag_recv, back_send,
    a_send, a_recv, c_send, c_recv, r_send, r_recv, g_send, g_recv, b_send, b_recv,
):
    devices = slabs * groups
    me = lax.axis_index("space")
    slab, group = me // groups, lax.rem(me, groups)
    offsets = slab_offsets(slabs)
    probe = K // groups
    cells = fields.shape[0] // probe
    width = cells // YS
    chunk = cells // groups

    barrier = pltpu.get_barrier_semaphore()
    for k in range(1, devices):
        pl.semaphore_signal(barrier, inc=1, device_id={"space": lax.rem(me + k, devices)}, device_id_type=MESH)

    field = jnp.stack([fields[pl.ds(c, probe, stride=cells), :] for c in range(cells)])
    field = field.reshape(width, YS, probe, 128)
    lane = lax.broadcasted_iota(jnp.int32, (probe, 128), 1)
    not_first, not_last = lane > 0, lane < 127

    def plane(u):
        flat = u.reshape(cells * probe, 128)
        low = pltpu.roll(flat, 1, 1).reshape(u.shape)
        high = pltpu.roll(flat, 127, 1).reshape(u.shape)
        total = jnp.where(not_first, low, 0.0) + jnp.where(not_last, high, 0.0)
        edge = jnp.zeros((1,) + u.shape[1:], u.dtype)
        return total + jnp.concatenate([u[1:], edge], 0) + jnp.concatenate([edge, u[:-1]], 0)

    d = 1.0 / 7.0
    one = plane(field)
    two = plane(one)
    three = plane(two)
    q0 = field * d + one * d**2 + two * d**3 + three * d**4
    q1 = field * d**2 + one * (2 * d**3) + two * (3 * d**4)
    q2 = field * d**3 + one * (3 * d**4)
    q3 = field * d**4

    def spread(other, own):
        rows = []
        for b in range(YS):
            a = 1 - b
            _, w2, _ = walks(YS * slab + b, YS * other + b, YS * slabs)
            w1, _, w3 = walks(YS * slab + a, YS * other + b, YS * slabs)
            value = w2 * q2[:, b] + w1 * q1[:, a] + w3 * q3[:, a]
            rows.append(q0[:, b] + value if own else value)
        return jnp.stack(rows, axis=1).reshape(groups, chunk, probe, 128)

    for n, offset in enumerate(offsets):
        cross_send[n] = spread(lax.rem(slab + offset, slabs), False)

    pl.semaphore_wait(barrier, devices - 1)

    started = []

    def send(src, dst, send_sem, recv_sem, peer):
        copy = pltpu.make_async_remote_copy(
            src_ref=src, dst_ref=dst, send_sem=send_sem, recv_sem=recv_sem,
            device_id={"space": peer}, device_id_type=MESH,
        )
        copy.start()
        started.append(copy)

    def arrive(dst, sem):
        pltpu.make_async_copy(dst, dst, sem).wait()

    for n, offset in enumerate(offsets):
        there = lax.rem(slab + offset, slabs)
        for k in range(groups):
            g = lax.rem(group + k, groups)
            send(cross_send.at[n, g], cross_recv.at[n, group], c_send.at[n, g], c_recv.at[n, group], there * groups + g)
    own_send[...] = spread(slab, True)
    for k in range(1, groups):
        g = lax.rem(group + k, groups)
        send(own_send.at[g], own_recv.at[group], a_send.at[g], a_recv.at[group], slab * groups + g)
    own_recv[group] = own_send[group]
    for k in range(1, groups):
        g = lax.rem(group + k, groups)
        arrive(own_recv.at[g], a_recv.at[g])
    for n in range(len(offsets)):
        for g in range(groups):
            arrive(cross_recv.at[n, g], c_recv.at[n, g])
    total = own_recv[...]
    for n in range(len(offsets)):
        total = total + cross_recv[n]
    matrix = jnp.concatenate([total[:, c].reshape(K, 128) for c in range(chunk)], axis=1)

    def summed(rows, turn, precision):
        part = lax.dot_general(
            rows, rows, (((1,), (1,)), ((), ())), precision=precision, preferred_element_type=jnp.float32
        )
        part = jnp.concatenate([part, jnp.zeros((K, 128 - K), jnp.float32)], axis=1)
        rs_send[turn] = part.reshape(groups, probe, 128)
        for k in range(1, devices):
            peer = lax.rem(me + k, devices)
            send(rs_send.at[turn, lax.rem(peer, groups)], rs_recv.at[turn, me], r_send.at[turn, peer], r_recv.at[turn, me], peer)
        rs_recv[turn, me] = rs_send[turn, group]
        for k in range(1, devices):
            peer = lax.rem(me + k, devices)
            arrive(rs_recv.at[turn, peer], r_recv.at[turn, peer])
        ag_send[turn] = jnp.sum(rs_recv[turn], axis=0)
        for k in range(1, groups):
            g = lax.rem(group + k, groups)
            send(ag_send.at[turn], ag_recv.at[turn, group], g_send.at[turn, g], g_recv.at[turn, group], slab * groups + g)
        ag_recv[turn, group] = ag_send[turn]
        for k in range(1, groups):
            g = lax.rem(group + k, groups)
            arrive(ag_recv.at[turn, g], g_recv.at[turn, g])
        return ag_recv[turn].reshape(K, 128)

    both_one = eliminate(summed(matrix, 0, highest))
    basis_one = jnp.dot(both_one[:, K:], matrix, precision=highest, preferred_element_type=jnp.float32)
    both_two = eliminate(summed(basis_one, 1, highest))
    basis = jnp.dot(both_two[:, K:] * scale, basis_one, precision=highest, preferred_element_type=jnp.float32)
    for c in range(chunk):
        back_send[:, c] = basis[:, 128 * c : 128 * c + 128].reshape(groups, probe, 128)
    for k in range(1, groups):
        g = lax.rem(group + k, groups)
        send(back_send.at[g], q_out.at[group], b_send.at[g], b_recv.at[group], slab * groups + g)
    q_out[group] = back_send[group]
    first = both_one[:, :K]
    first_out[...] = first * (1.0 / scale)
    r_out[...] = jnp.dot(both_two[:, :K], first, precision=highest, preferred_element_type=jnp.float32) * (1.0 / scale)
    for k in range(1, groups):
        g = lax.rem(group + k, groups)
        arrive(q_out.at[g], b_recv.at[g])
    for copy in started:
        copy.wait_send()


def shards(actions):
    _, probe, width, rows_y, depth = actions.shape
    devices = lax.axis_size("space")
    groups = K // probe
    slabs = devices // groups
    cells = width * rows_y
    chunk = cells // groups
    others = len(slab_offsets(slabs))
    scale = math.sqrt(width * rows_y * slabs * depth)
    dma = pltpu.SemaphoreType.DMA
    block = (groups, chunk, probe, depth)
    f32 = jnp.float32
    vmem = pl.BlockSpec(memory_space=pltpu.VMEM)
    q, r, first = pl.pallas_call(
        functools.partial(kernel, slabs, groups, scale),
        out_shape=(
            jax.ShapeDtypeStruct(block, f32),
            jax.ShapeDtypeStruct((K, K), f32),
            jax.ShapeDtypeStruct((K, K), f32),
        ),
        in_specs=[vmem],
        out_specs=(vmem, vmem, vmem),
        scratch_shapes=[
            pltpu.VMEM(block, f32),
            pltpu.VMEM((others,) + block, f32),
            pltpu.VMEM(block, f32),
            pltpu.VMEM((others,) + block, f32),
            pltpu.VMEM((2, groups, probe, 128), f32),
            pltpu.VMEM((2, devices, probe, 128), f32),
            pltpu.VMEM((2, probe, 128), f32),
            pltpu.VMEM((2, groups, probe, 128), f32),
            pltpu.VMEM(block, f32),
            dma((groups,)), dma((groups,)),
            dma((others, groups)), dma((others, groups)),
            dma((2, devices)), dma((2, devices)),
            dma((2, groups)), dma((2, groups)),
            dma((groups,)), dma((groups,)),
        ],
        compiler_params=pltpu.CompilerParams(
            collective_id=0, has_side_effects=True, vmem_limit_bytes=48 * 1024 * 1024
        ),
    )(actions.reshape(probe * cells, depth))
    q_fields = q.reshape(cells, probe, depth).transpose(1, 0, 2)
    return (q_fields.reshape(1, probe, width, rows_y, depth), r, first)


def solution(mesh):
    in_specs = (P(("groups", "space"), None, None, None, None),)
    out_specs = (
        P(("groups", "space"), None, None, None, None),
        P("groups", None),
        P("groups", None),
    )
    return jax.shard_map(shards, mesh=mesh, in_specs=in_specs, out_specs=out_specs, check_vma=False)
```

```python
import functools
import math

import jax
import jax.numpy as jnp
from jax import lax
from jax.experimental import pallas as pl
from jax.experimental.pallas import tpu as pltpu
from jax.sharding import PartitionSpec as P

K = 64
YS = 2
highest = lax.Precision.HIGHEST
MESH = pl.DeviceIdType.MESH


def slab_offsets(slabs):
    return sorted({d % slabs for d in (1, -1, 2, -2)} - {0})


def walks(p, q, rows):
    gap = jnp.abs(p - q)
    low, high = jnp.minimum(p, q), jnp.maximum(p, q)
    at_start = jnp.where(low == 0, 1, 0)
    at_end = jnp.where(high == rows - 1, 1, 0)
    one = jnp.where(gap == 1, 1, 0)
    two = jnp.where(gap == 2, 1, 0) + jnp.where(gap == 0, 2 - at_start - at_end, 0)
    three = jnp.where(gap == 3, 1, 0) + jnp.where(gap == 1, 3 - at_start - at_end, 0)
    return one.astype(jnp.float32), two.astype(jnp.float32), three.astype(jnp.float32)


def eliminate(gram):
    lane = lax.broadcasted_iota(jnp.int32, (K, 128), 1)
    row_id = lax.broadcasted_iota(jnp.int32, (K, 128), 0)
    full = jnp.concatenate([gram, pltpu.roll(gram, K, 1)], axis=0)
    full = jnp.where(lane < K, full, jnp.where(lane - K == row_id, 1.0, 0.0))
    blocks = [full[8 * i : 8 * i + 8] for i in range(K // 8)]
    sub = lax.broadcasted_iota(jnp.int32, (8, 128), 0)
    count = len(blocks)
    shape = (8, 128)
    scaled = []
    for t in range(count):
        cols = [
            {i: jnp.broadcast_to(blocks[i][:, 8 * t + k : 8 * t + k + 1], shape) for i in range(t, count)}
            for k in range(8)
        ]
        pivots = jnp.ones(shape, jnp.float32)
        for r in range(8):
            pivot = jnp.broadcast_to(cols[r][t][r : r + 1], shape)
            pivots = jnp.where(sub == r, pivot, pivots)
            inverse = 1.0 / pivot
            factors = {i: cols[r][i] * inverse for i in range(t, count)}
            factors[t] = jnp.where(sub > r, factors[t], 0.0)
            for k in range(r + 1, 8):
                value = jnp.broadcast_to(cols[r][t][k : k + 1], shape)
                for i in range(t, count):
                    cols[k][i] = cols[k][i] - factors[i] * value
            row = jnp.broadcast_to(blocks[t][r : r + 1], shape)
            for i in range(t, count):
                blocks[i] = blocks[i] - factors[i] * row
        scaled.append(blocks[t] * lax.rsqrt(pivots))
    done = jnp.concatenate(scaled, axis=0)
    offset = jnp.where(lane < K, lane - row_id, row_id + K - lane)
    return jnp.where(offset >= 0, done, 0.0)


def kernel(
    slabs, groups, scale,
    source, q_out, factors_out,
    fields,
    own_send, cross_send, own_recv, cross_recv, part_send, part_recv, half_send, half_recv, back_send,
    a_send, a_recv, c_send, c_recv, p_send, p_recv, h_send, h_recv, b_send, b_recv, in_sem,
):
    devices = slabs * groups
    me = lax.axis_index("space")
    slab, group = me // groups, lax.rem(me, groups)
    offsets = slab_offsets(slabs)
    probe = K // groups
    cells = fields.shape[0] // probe
    width = cells // YS
    chunk = cells // groups

    core = lax.rem(me, 2)
    load = pltpu.make_async_copy(source, fields, in_sem)
    load.start()
    barrier = pltpu.get_barrier_semaphore()
    for k in range(1, devices):
        pl.semaphore_signal(barrier, inc=1, device_id={"space": lax.rem(me + k, devices)}, device_id_type=MESH)

    load.wait()
    field = jnp.stack([fields[pl.ds(c, probe, stride=cells), :] for c in range(cells)])
    field = field.reshape(width, YS, probe, 128)
    lane = lax.broadcasted_iota(jnp.int32, (probe, 128), 1)
    not_first, not_last = lane > 0, lane < 127

    def plane(u):
        flat = u.reshape(cells * probe, 128)
        low = pltpu.roll(flat, 1, 1).reshape(u.shape)
        high = pltpu.roll(flat, 127, 1).reshape(u.shape)
        total = jnp.where(not_first, low, 0.0) + jnp.where(not_last, high, 0.0)
        edge = jnp.zeros((1,) + u.shape[1:], u.dtype)
        return total + jnp.concatenate([u[1:], edge], 0) + jnp.concatenate([edge, u[:-1]], 0)

    d = 1.0 / 7.0
    one = plane(field)
    two = plane(one)
    three = plane(two)
    q0 = field * d + one * d**2 + two * d**3 + three * d**4
    q1 = field * d**2 + one * (2 * d**3) + two * (3 * d**4)
    q2 = field * d**3 + one * (3 * d**4)
    q3 = field * d**4

    def spread(other, own):
        rows = []
        for b in range(YS):
            a = 1 - b
            _, w2, _ = walks(YS * slab + b, YS * other + b, YS * slabs)
            w1, _, w3 = walks(YS * slab + a, YS * other + b, YS * slabs)
            value = w2 * q2[:, b] + w1 * q1[:, a] + w3 * q3[:, a]
            rows.append(q0[:, b] + value if own else value)
        return jnp.stack(rows, axis=1).reshape(groups, chunk, probe, 128)

    for n, offset in enumerate(offsets):
        cross_send[n] = spread(lax.rem(slab + offset, slabs), False)

    pl.semaphore_wait(barrier, devices - 1)

    started = []

    def send(src, dst, send_sem, recv_sem, peer):
        copy = pltpu.make_async_remote_copy(
            src_ref=src, dst_ref=dst, send_sem=send_sem, recv_sem=recv_sem,
            device_id={"space": peer}, device_id_type=MESH,
        )
        copy.start()
        started.append(copy)

    def arrive(dst, sem):
        pltpu.make_async_copy(dst, dst, sem).wait()

    for n, offset in enumerate(offsets):
        there = lax.rem(slab + offset, slabs)
        for k in range(groups):
            g = lax.rem(group + k, groups)
            send(cross_send.at[n, g], cross_recv.at[n, group], c_send.at[n, g], c_recv.at[n, group], there * groups + g)
    own_send[...] = spread(slab, True)
    for k in range(1, groups):
        g = lax.rem(group + k, groups)
        send(own_send.at[g], own_recv.at[group], a_send.at[g], a_recv.at[group], slab * groups + g)
    own_recv[group] = own_send[group]
    for k in range(1, groups):
        g = lax.rem(group + k, groups)
        arrive(own_recv.at[g], a_recv.at[g])
    for n in range(len(offsets)):
        for g in range(groups):
            arrive(cross_recv.at[n, g], c_recv.at[n, g])
    total = own_recv[...]
    for n in range(len(offsets)):
        total = total + cross_recv[n]
    matrix = jnp.concatenate([total[:, c].reshape(K, 128) for c in range(chunk)], axis=1)

    def summed(rows, turn, precision):
        part = lax.dot_general(
            rows, rows, (((1,), (1,)), ((), ())), precision=precision, preferred_element_type=jnp.float32
        )
        part = jnp.concatenate([part[: K // 2], part[K // 2 :]], axis=1)
        part_send[turn] = part.reshape(2, K // 4, 128)
        send(part_send.at[turn, 1 - core], part_recv.at[turn], p_send.at[turn], p_recv.at[turn], me + 1 - 2 * core)
        arrive(part_recv.at[turn], p_recv.at[turn])
        half_send[turn] = part_send[turn, core] + part_recv[turn]
        for k in reversed(range(1, devices)):
            peer = lax.rem(me + k, devices)
            send(half_send.at[turn], half_recv.at[turn, me], h_send.at[turn, peer], h_recv.at[turn, me], peer)
        half_recv[turn, me] = half_send[turn]
        for k in range(1, devices):
            peer = lax.rem(me + k, devices)
            arrive(half_recv.at[turn, peer], h_recv.at[turn, peer])
        return jnp.sum(half_recv[turn].reshape(devices // 2, K // 2, 128), axis=0)

    both_one = eliminate(summed(matrix, 0, highest))
    basis_one = jnp.dot(both_one[:, K:], matrix, precision=highest, preferred_element_type=jnp.float32)
    both_two = eliminate(summed(basis_one, 1, highest))
    basis = jnp.dot(both_two[:, K:] * scale, basis_one, precision=highest, preferred_element_type=jnp.float32)
    for c in range(chunk):
        back_send[:, c] = basis[:, 128 * c : 128 * c + 128].reshape(groups, probe, 128)
    for k in range(1, groups):
        g = lax.rem(group + k, groups)
        send(back_send.at[g], q_out.at[group], b_send.at[g], b_recv.at[group], slab * groups + g)
    q_out[group] = back_send[group]
    first = both_one[:, :K]
    r = jnp.dot(both_two[:, :K], first, precision=highest, preferred_element_type=jnp.float32)
    factors_out[...] = jnp.concatenate([r, first], axis=1) * (1.0 / scale)
    for k in range(1, groups):
        g = lax.rem(group + k, groups)
        arrive(q_out.at[g], b_recv.at[g])
    for copy in started:
        copy.wait_send()


def shards(actions):
    _, probe, width, rows_y, depth = actions.shape
    devices = lax.axis_size("space")
    groups = K // probe
    slabs = devices // groups
    cells = width * rows_y
    chunk = cells // groups
    others = len(slab_offsets(slabs))
    scale = math.sqrt(width * rows_y * slabs * depth)
    dma = pltpu.SemaphoreType.DMA
    block = (groups, chunk, probe, depth)
    f32 = jnp.float32
    vmem = pl.BlockSpec(memory_space=pltpu.VMEM)
    q, factors = pl.pallas_call(
        functools.partial(kernel, slabs, groups, scale),
        out_shape=(
            jax.ShapeDtypeStruct(block, f32),
            jax.ShapeDtypeStruct((K, 2 * K), f32),
        ),
        in_specs=[pl.BlockSpec(memory_space=pl.ANY)],
        out_specs=(vmem, vmem),
        scratch_shapes=[
            pltpu.VMEM((probe * cells, depth), f32),
            pltpu.VMEM(block, f32),
            pltpu.VMEM((others,) + block, f32),
            pltpu.VMEM(block, f32),
            pltpu.VMEM((others,) + block, f32),
            pltpu.VMEM((2, 2, K // 4, 128), f32),
            pltpu.VMEM((2, K // 4, 128), f32),
            pltpu.VMEM((2, K // 4, 128), f32),
            pltpu.VMEM((2, devices, K // 4, 128), f32),
            pltpu.VMEM(block, f32),
            dma((groups,)), dma((groups,)),
            dma((others, groups)), dma((others, groups)),
            dma((2,)), dma((2,)),
            dma((2, devices)), dma((2, devices)),
            dma((groups,)), dma((groups,)),
            dma(()),
        ],
        compiler_params=pltpu.CompilerParams(
            collective_id=0, has_side_effects=True, vmem_limit_bytes=60 * 1024 * 1024
        ),
    )(actions.reshape(probe * cells, depth))
    q_fields = q.reshape(cells, probe, depth).transpose(1, 0, 2)
    return (q_fields.reshape(1, probe, width, rows_y, depth), factors[:, :K], factors[:, K:])


def solution(mesh):
    in_specs = (P(("groups", "space"), None, None, None, None),)
    out_specs = (
        P(("groups", "space"), None, None, None, None),
        P("groups", None),
        P("groups", None),
    )
    return jax.shard_map(shards, mesh=mesh, in_specs=in_specs, out_specs=out_specs, check_vma=False)
```

```python
import functools
import math

import jax
import jax.numpy as jnp
from jax import lax
from jax.experimental import pallas as pl
from jax.experimental.pallas import tpu as pltpu
from jax.sharding import PartitionSpec as P

K = 64
YS = 2
highest = lax.Precision.HIGHEST
MESH = pl.DeviceIdType.MESH


def slab_offsets(slabs):
    return sorted({d % slabs for d in (1, -1, 2, -2)} - {0})


def walks(p, q, rows):
    gap = jnp.abs(p - q)
    low, high = jnp.minimum(p, q), jnp.maximum(p, q)
    at_start = jnp.where(low == 0, 1, 0)
    at_end = jnp.where(high == rows - 1, 1, 0)
    one = jnp.where(gap == 1, 1, 0)
    two = jnp.where(gap == 2, 1, 0) + jnp.where(gap == 0, 2 - at_start - at_end, 0)
    three = jnp.where(gap == 3, 1, 0) + jnp.where(gap == 1, 3 - at_start - at_end, 0)
    return one.astype(jnp.float32), two.astype(jnp.float32), three.astype(jnp.float32)


def eliminate(gram):
    lane = lax.broadcasted_iota(jnp.int32, (K, 128), 1)
    row_id = lax.broadcasted_iota(jnp.int32, (K, 128), 0)
    full = jnp.concatenate([gram, pltpu.roll(gram, K, 1)], axis=0)
    full = jnp.where(lane < K, full, jnp.where(lane - K == row_id, 1.0, 0.0))
    blocks = [full[8 * i : 8 * i + 8] for i in range(K // 8)]
    sub = lax.broadcasted_iota(jnp.int32, (8, 128), 0)
    count = len(blocks)
    shape = (8, 128)
    scaled = []
    for t in range(count):
        cols = [
            {i: jnp.broadcast_to(blocks[i][:, 8 * t + k : 8 * t + k + 1], shape) for i in range(t, count)}
            for k in range(8)
        ]
        pivots = jnp.ones(shape, jnp.float32)
        for r in range(8):
            pivot = jnp.broadcast_to(cols[r][t][r : r + 1], shape)
            pivots = jnp.where(sub == r, pivot, pivots)
            inverse = 1.0 / pivot
            factors = {i: cols[r][i] * inverse for i in range(t, count)}
            factors[t] = jnp.where(sub > r, factors[t], 0.0)
            for k in range(r + 1, 8):
                value = jnp.broadcast_to(cols[r][t][k : k + 1], shape)
                for i in range(t, count):
                    cols[k][i] = cols[k][i] - factors[i] * value
            row = jnp.broadcast_to(blocks[t][r : r + 1], shape)
            for i in range(t, count):
                blocks[i] = blocks[i] - factors[i] * row
        scaled.append(blocks[t] * lax.rsqrt(pivots))
    done = jnp.concatenate(scaled, axis=0)
    offset = jnp.where(lane < K, lane - row_id, row_id + K - lane)
    return jnp.where(offset >= 0, done, 0.0)


def kernel(
    slabs, groups, scale,
    source, q_out, factors_out,
    fields,
    own_send, cross_send, own_recv, cross_recv, part_send, part_recv, half_send, half_recv, mine, slab_rows, inverses,
    a_send, a_recv, c_send, c_recv, p_send, p_recv, h_send, h_recv, b_send, b_recv, in_sem,
):
    devices = slabs * groups
    me = lax.axis_index("space")
    slab, group = me // groups, lax.rem(me, groups)
    offsets = slab_offsets(slabs)
    probe = K // groups
    cells = fields.shape[0] // probe
    width = cells // YS
    chunk = cells // groups

    core = lax.rem(me, 2)
    load = pltpu.make_async_copy(source, fields, in_sem)
    load.start()
    barrier = pltpu.get_barrier_semaphore()
    for k in range(1, devices):
        pl.semaphore_signal(barrier, inc=1, device_id={"space": lax.rem(me + k, devices)}, device_id_type=MESH)

    load.wait()
    field = jnp.stack([fields[pl.ds(c, probe, stride=cells), :] for c in range(cells)])
    field = field.reshape(width, YS, probe, 128)
    lane = lax.broadcasted_iota(jnp.int32, (probe, 128), 1)
    not_first, not_last = lane > 0, lane < 127

    def plane(u):
        flat = u.reshape(cells * probe, 128)
        low = pltpu.roll(flat, 1, 1).reshape(u.shape)
        high = pltpu.roll(flat, 127, 1).reshape(u.shape)
        total = jnp.where(not_first, low, 0.0) + jnp.where(not_last, high, 0.0)
        edge = jnp.zeros((1,) + u.shape[1:], u.dtype)
        return total + jnp.concatenate([u[1:], edge], 0) + jnp.concatenate([edge, u[:-1]], 0)

    d = 1.0 / 7.0
    one = plane(field)
    two = plane(one)
    three = plane(two)
    q0 = field * d + one * d**2 + two * d**3 + three * d**4
    q1 = field * d**2 + one * (2 * d**3) + two * (3 * d**4)
    q2 = field * d**3 + one * (3 * d**4)
    q3 = field * d**4

    def spread(other, own):
        rows = []
        for b in range(YS):
            a = 1 - b
            _, w2, _ = walks(YS * slab + b, YS * other + b, YS * slabs)
            w1, _, w3 = walks(YS * slab + a, YS * other + b, YS * slabs)
            value = w2 * q2[:, b] + w1 * q1[:, a] + w3 * q3[:, a]
            rows.append(q0[:, b] + value if own else value)
        return jnp.stack(rows, axis=1).reshape(groups, chunk, probe, 128)

    for n, offset in enumerate(offsets):
        cross_send[n] = spread(lax.rem(slab + offset, slabs), False)

    pl.semaphore_wait(barrier, devices - 1)

    started = []

    def send(src, dst, send_sem, recv_sem, peer):
        copy = pltpu.make_async_remote_copy(
            src_ref=src, dst_ref=dst, send_sem=send_sem, recv_sem=recv_sem,
            device_id={"space": peer}, device_id_type=MESH,
        )
        copy.start()
        started.append(copy)

    def arrive(dst, sem):
        pltpu.make_async_copy(dst, dst, sem).wait()

    for n, offset in enumerate(offsets):
        there = lax.rem(slab + offset, slabs)
        for k in range(groups):
            g = lax.rem(group + k, groups)
            send(cross_send.at[n, g], cross_recv.at[n, group], c_send.at[n, g], c_recv.at[n, group], there * groups + g)
    own_send[...] = spread(slab, True)
    for k in range(1, groups):
        g = lax.rem(group + k, groups)
        send(own_send.at[g], own_recv.at[group], a_send.at[g], a_recv.at[group], slab * groups + g)
    own_recv[group] = own_send[group]
    for k in range(1, groups):
        g = lax.rem(group + k, groups)
        arrive(own_recv.at[g], a_recv.at[g])
    for n in range(len(offsets)):
        for g in range(groups):
            arrive(cross_recv.at[n, g], c_recv.at[n, g])
    total = own_recv[...]
    for n in range(len(offsets)):
        total = total + cross_recv[n]
    for c in range(chunk):
        mine[c] = total[:, c].reshape(K, 128)
    matrix = jnp.concatenate([mine[c] for c in range(chunk)], axis=1)

    beside_me = 1 - 2 * core

    def share():
        for k in reversed(range(2, groups, 2)):
            g = lax.rem(group + k, groups)
            send(mine, slab_rows.at[group], b_send.at[g], b_recv.at[group], slab * groups + g)
        g = group + beside_me
        send(mine, slab_rows.at[group], b_send.at[g], b_recv.at[group], slab * groups + g)
        slab_rows[group] = mine[...]

    def relay():
        for k in range(2, groups, 2):
            g = lax.rem(group + k, groups)
            arrive(slab_rows.at[g], b_recv.at[g])
            send(slab_rows.at[g], slab_rows.at[g], b_send.at[g + beside_me], b_recv.at[g], me + beside_me)

    def summed(rows, turn, beside):
        part = lax.dot_general(
            rows, rows, (((1,), (1,)), ((), ())), precision=highest, preferred_element_type=jnp.float32
        )
        part = jnp.concatenate([part[: K // 2], part[K // 2 :]], axis=1)
        part_send[turn] = part.reshape(2, K // 4, 128)
        send(part_send.at[turn, 1 - core], part_recv.at[turn], p_send.at[turn], p_recv.at[turn], me + 1 - 2 * core)
        arrive(part_recv.at[turn], p_recv.at[turn])
        half_send[turn] = part_send[turn, core] + part_recv[turn]
        for k in reversed(range(1, devices)):
            peer = lax.rem(me + k, devices)
            send(half_send.at[turn], half_recv.at[turn, me], h_send.at[turn, peer], h_recv.at[turn, me], peer)
        half_recv[turn, me] = half_send[turn]
        beside()
        for k in range(1, devices):
            peer = lax.rem(me + k, devices)
            arrive(half_recv.at[turn, peer], h_recv.at[turn, peer])
        return jnp.sum(half_recv[turn].reshape(devices // 2, K // 2, 128), axis=0)

    both_one = eliminate(summed(matrix, 0, share))
    basis_one = jnp.dot(both_one[:, K:], matrix, precision=highest, preferred_element_type=jnp.float32)
    both_two = eliminate(summed(basis_one, 1, relay))
    product = jnp.dot(both_two[:, K:] * scale, both_one[:, K:], precision=highest, preferred_element_type=jnp.float32)
    inverses[:, :K] = product
    weights = inverses[pl.ds(pl.multiple_of(group * probe, probe), probe), :][:, :K]
    for k in range(0, groups, 2):
        g = lax.rem(group + k, groups) + beside_me
        arrive(slab_rows.at[g], b_recv.at[g])
    for g in range(groups):
        rows = jnp.concatenate([slab_rows[g, c] for c in range(chunk)], axis=1)
        basis = jnp.dot(weights, rows, precision=highest, preferred_element_type=jnp.float32)
        for c in range(chunk):
            q_out[g, c] = basis[:, 128 * c : 128 * c + 128]
    first = both_one[:, :K]
    r = jnp.dot(both_two[:, :K], first, precision=highest, preferred_element_type=jnp.float32)
    factors_out[...] = jnp.concatenate([r, first], axis=1) * (1.0 / scale)
    for copy in started:
        copy.wait_send()


def shards(actions):
    _, probe, width, rows_y, depth = actions.shape
    devices = lax.axis_size("space")
    groups = K // probe
    slabs = devices // groups
    cells = width * rows_y
    chunk = cells // groups
    others = len(slab_offsets(slabs))
    scale = math.sqrt(width * rows_y * slabs * depth)
    dma = pltpu.SemaphoreType.DMA
    block = (groups, chunk, probe, depth)
    f32 = jnp.float32
    vmem = pl.BlockSpec(memory_space=pltpu.VMEM)
    q, factors = pl.pallas_call(
        functools.partial(kernel, slabs, groups, scale),
        out_shape=(
            jax.ShapeDtypeStruct(block, f32),
            jax.ShapeDtypeStruct((K, 2 * K), f32),
        ),
        in_specs=[pl.BlockSpec(memory_space=pltpu.HBM)],
        out_specs=(vmem, vmem),
        scratch_shapes=[
            pltpu.VMEM((probe * cells, depth), f32),
            pltpu.VMEM(block, f32),
            pltpu.VMEM((others,) + block, f32),
            pltpu.VMEM(block, f32),
            pltpu.VMEM((others,) + block, f32),
            pltpu.VMEM((2, 2, K // 4, 128), f32),
            pltpu.VMEM((2, K // 4, 128), f32),
            pltpu.VMEM((2, K // 4, 128), f32),
            pltpu.VMEM((2, devices, K // 4, 128), f32),
            pltpu.VMEM((chunk, K, depth), f32),
            pltpu.VMEM((groups, chunk, K, depth), f32),
            pltpu.VMEM((K, 128), f32),
            dma((groups,)), dma((groups,)),
            dma((others, groups)), dma((others, groups)),
            dma((2,)), dma((2,)),
            dma((2, devices)), dma((2, devices)),
            dma((groups,)), dma((groups,)),
            dma(()),
        ],
        compiler_params=pltpu.CompilerParams(
            collective_id=0, has_side_effects=True, vmem_limit_bytes=20 * 1024 * 1024 + 16 * 4 * math.prod(block)
        ),
    )(actions.reshape(probe * cells, depth))
    q_fields = q.reshape(cells, probe, depth).transpose(1, 0, 2)
    return (q_fields.reshape(1, probe, width, rows_y, depth), factors[:, :K], factors[:, K:])


def solution(mesh):
    in_specs = (P(("groups", "space"), None, None, None, None),)
    out_specs = (
        P(("groups", "space"), None, None, None, None),
        P("groups", None),
        P("groups", None),
    )
    return jax.shard_map(shards, mesh=mesh, in_specs=in_specs, out_specs=out_specs, check_vma=False)
```

```python
import functools
import math

import jax
import jax.numpy as jnp
from jax import lax
from jax.experimental import pallas as pl
from jax.experimental.pallas import tpu as pltpu
from jax.sharding import PartitionSpec as P

K = 64
YS = 2
highest = lax.Precision.HIGHEST
MESH = pl.DeviceIdType.MESH


def slab_offsets(slabs):
    return sorted({d % slabs for d in (1, -1, 2, -2)} - {0})


def walks(p, q, rows):
    gap = jnp.abs(p - q)
    low, high = jnp.minimum(p, q), jnp.maximum(p, q)
    at_start = jnp.where(low == 0, 1, 0)
    at_end = jnp.where(high == rows - 1, 1, 0)
    one = jnp.where(gap == 1, 1, 0)
    two = jnp.where(gap == 2, 1, 0) + jnp.where(gap == 0, 2 - at_start - at_end, 0)
    three = jnp.where(gap == 3, 1, 0) + jnp.where(gap == 1, 3 - at_start - at_end, 0)
    return one.astype(jnp.float32), two.astype(jnp.float32), three.astype(jnp.float32)


def eliminate(gram):
    lane = lax.broadcasted_iota(jnp.int32, (K, 128), 1)
    row_id = lax.broadcasted_iota(jnp.int32, (K, 128), 0)
    full = jnp.concatenate([gram, pltpu.roll(gram, K, 1)], axis=0)
    full = jnp.where(lane < K, full, jnp.where(lane - K == row_id, 1.0, 0.0))
    blocks = [full[8 * i : 8 * i + 8] for i in range(K // 8)]
    sub = lax.broadcasted_iota(jnp.int32, (8, 128), 0)
    count = len(blocks)
    shape = (8, 128)
    scaled = []
    for t in range(count):
        cols = [
            {i: jnp.broadcast_to(blocks[i][:, 8 * t + k : 8 * t + k + 1], shape) for i in range(t, count)}
            for k in range(8)
        ]
        pivots = jnp.ones(shape, jnp.float32)
        for r in range(8):
            pivot = jnp.broadcast_to(cols[r][t][r : r + 1], shape)
            pivots = jnp.where(sub == r, pivot, pivots)
            inverse = 1.0 / pivot
            factors = {i: cols[r][i] * inverse for i in range(t, count)}
            factors[t] = jnp.where(sub > r, factors[t], 0.0)
            for k in range(r + 1, 8):
                value = jnp.broadcast_to(cols[r][t][k : k + 1], shape)
                for i in range(t, count):
                    cols[k][i] = cols[k][i] - factors[i] * value
            row = jnp.broadcast_to(blocks[t][r : r + 1], shape)
            for i in range(t, count):
                blocks[i] = blocks[i] - factors[i] * row
        scaled.append(blocks[t] * lax.rsqrt(pivots))
    done = jnp.concatenate(scaled, axis=0)
    offset = jnp.where(lane < K, lane - row_id, row_id + K - lane)
    return jnp.where(offset >= 0, done, 0.0)


def kernel(
    slabs, groups, scale,
    source, q_out, factors_out,
    fields,
    own_send, cross_send, own_recv, cross_recv, part_send, part_recv, half_send, half_recv, mine, slab_rows, inverses, pair_rows,
    a_send, a_recv, c_send, c_recv, p_send, p_recv, h_send, h_recv, b_send, b_recv, in_sem,
):
    devices = slabs * groups
    me = lax.axis_index("space")
    slab, group = me // groups, lax.rem(me, groups)
    offsets = slab_offsets(slabs)
    probe = K // groups
    cells = fields.shape[0] // probe
    width = cells // YS
    chunk = cells // groups

    core = lax.rem(me, 2)
    load = pltpu.make_async_copy(source, fields, in_sem)
    load.start()
    barrier = pltpu.get_barrier_semaphore()
    for k in reversed(range(1, devices)):
        pl.semaphore_signal(barrier, inc=1, device_id={"space": lax.rem(me + k, devices)}, device_id_type=MESH)

    load.wait()
    field = jnp.stack([fields[pl.ds(c, probe, stride=cells), :] for c in range(cells)])
    field = field.reshape(width, YS, probe, 128)
    lane = lax.broadcasted_iota(jnp.int32, (probe, 128), 1)
    not_first, not_last = lane > 0, lane < 127

    def plane(u):
        flat = u.reshape(cells * probe, 128)
        low = pltpu.roll(flat, 1, 1).reshape(u.shape)
        high = pltpu.roll(flat, 127, 1).reshape(u.shape)
        total = jnp.where(not_first, low, 0.0) + jnp.where(not_last, high, 0.0)
        edge = jnp.zeros((1,) + u.shape[1:], u.dtype)
        return total + jnp.concatenate([u[1:], edge], 0) + jnp.concatenate([edge, u[:-1]], 0)

    d = 1.0 / 7.0
    one = plane(field)
    two = plane(one)
    three = plane(two)
    q0 = field * d + one * d**2 + two * d**3 + three * d**4
    q1 = field * d**2 + one * (2 * d**3) + two * (3 * d**4)
    q2 = field * d**3 + one * (3 * d**4)
    q3 = field * d**4

    def spread(other, own):
        rows = []
        for b in range(YS):
            a = 1 - b
            _, w2, _ = walks(YS * slab + b, YS * other + b, YS * slabs)
            w1, _, w3 = walks(YS * slab + a, YS * other + b, YS * slabs)
            value = w2 * q2[:, b] + w1 * q1[:, a] + w3 * q3[:, a]
            rows.append(q0[:, b] + value if own else value)
        return jnp.stack(rows, axis=1).reshape(groups, chunk, probe, 128)

    for n, offset in enumerate(offsets):
        cross_send[n] = spread(lax.rem(slab + offset, slabs), False)

    pl.semaphore_wait(barrier, devices - 1)

    started = []

    def send(src, dst, send_sem, recv_sem, peer):
        copy = pltpu.make_async_remote_copy(
            src_ref=src, dst_ref=dst, send_sem=send_sem, recv_sem=recv_sem,
            device_id={"space": peer}, device_id_type=MESH,
        )
        copy.start()
        started.append(copy)

    def drain(limit):
        while len(started) > limit:
            started.pop(0).wait_send()

    def arrive(dst, sem):
        pltpu.make_async_copy(dst, dst, sem).wait()

    for n, offset in enumerate(offsets):
        there = lax.rem(slab + offset, slabs)
        for k in range(groups):
            g = lax.rem(group + k, groups)
            send(cross_send.at[n, g], cross_recv.at[n, group], c_send.at[n, g], c_recv.at[n, group], there * groups + g)
    own_send[...] = spread(slab, True)
    for k in range(1, groups):
        g = lax.rem(group + k, groups)
        send(own_send.at[g], own_recv.at[group], a_send.at[g], a_recv.at[group], slab * groups + g)
    own_recv[group] = own_send[group]
    for k in range(1, groups):
        g = lax.rem(group + k, groups)
        arrive(own_recv.at[g], a_recv.at[g])
    for n in range(len(offsets)):
        for g in range(groups):
            arrive(cross_recv.at[n, g], c_recv.at[n, g])
    total = own_recv[...]
    for n in range(len(offsets)):
        total = total + cross_recv[n]
    for c in range(chunk):
        mine[c] = total[:, c].reshape(K, 128)
    matrix = jnp.concatenate([mine[c] for c in range(chunk)], axis=1)

    beside_me = 1 - 2 * core

    def share():
        for k in reversed(range(2, groups, 2)):
            g = lax.rem(group + k, groups)
            send(mine, slab_rows.at[group], b_send.at[g], b_recv.at[group], slab * groups + g)
        g = group + beside_me
        send(mine, slab_rows.at[group], b_send.at[g], b_recv.at[group], slab * groups + g)
        slab_rows[group] = mine[...]

    def relay():
        for k in range(2, groups, 2):
            g = lax.rem(group + k, groups)
            arrive(slab_rows.at[g], b_recv.at[g])
            send(slab_rows.at[g], slab_rows.at[g], b_send.at[g + beside_me], b_recv.at[g], me + beside_me)

    def summed(rows):
        before = len(started)
        part = lax.dot_general(
            rows, rows, (((1,), (1,)), ((), ())), precision=highest, preferred_element_type=jnp.float32
        )
        part = jnp.concatenate([part[: K // 2], part[K // 2 :]], axis=1)
        part_send[...] = part.reshape(2, K // 4, 128)
        send(part_send.at[1 - core], part_recv, p_send, p_recv, me + beside_me)
        arrive(part_recv, p_recv)
        return added(part_send[core] + part_recv[...], 0, share, before)

    def added(half, turn, beside, before):
        half_send[turn] = half
        for k in reversed(range(1, devices)):
            peer = lax.rem(me + k, devices)
            send(half_send.at[turn], half_recv.at[turn, me], h_send.at[turn, peer], h_recv.at[turn, me], peer)
        half_recv[turn, me] = half_send[turn]
        beside()
        drain(len(started) - before)
        for k in range(1, devices):
            peer = lax.rem(me + k, devices)
            arrive(half_recv.at[turn, peer], h_recv.at[turn, peer])
        return jnp.sum(half_recv[turn].reshape(devices // 2, K // 2, 128), axis=0)

    both_one = eliminate(summed(matrix))
    beside = group + beside_me
    arrive(slab_rows.at[beside], b_recv.at[beside])
    pair = jnp.concatenate([matrix] + [slab_rows[beside, c] for c in range(chunk)], axis=1)
    basis_one = jnp.dot(both_one[:, K:], pair, precision=highest, preferred_element_type=jnp.float32)
    pair_rows[...] = basis_one
    quarter = K // 4
    low = pl.multiple_of(core * quarter, quarter)
    mine_low, mine_high = pair_rows[pl.ds(low, quarter), :], pair_rows[pl.ds(low + K // 2, quarter), :]
    part = lax.dot_general(
        jnp.concatenate([mine_low, mine_high], axis=0), basis_one, (((1,), (1,)), ((), ())),
        precision=highest, preferred_element_type=jnp.float32,
    )
    part = jnp.concatenate([part[:quarter], part[quarter:]], axis=1)
    both_two = eliminate(added(part, 1, relay, len(started)))
    product = jnp.dot(both_two[:, K:] * scale, both_one[:, K:], precision=highest, preferred_element_type=jnp.float32)
    inverses[:, :K] = product
    weights = inverses[pl.ds(pl.multiple_of(group * probe, probe), probe), :][:, :K]
    for k in range(2, groups, 2):
        g = lax.rem(group + k, groups) + beside_me
        arrive(slab_rows.at[g], b_recv.at[g])
    for g in range(groups):
        rows = jnp.concatenate([slab_rows[g, c] for c in range(chunk)], axis=1)
        basis = jnp.dot(weights, rows, precision=highest, preferred_element_type=jnp.float32)
        for c in range(chunk):
            q_out[g, c] = basis[:, 128 * c : 128 * c + 128]
    first = both_one[:, :K]
    r = jnp.dot(both_two[:, :K], first, precision=highest, preferred_element_type=jnp.float32)
    factors_out[...] = jnp.concatenate([r, first], axis=1) * (1.0 / scale)
    drain(0)


def finish(blocks, factors, q_out, r_out, first_out):
    cells, probe, _ = blocks.shape
    for c in range(cells):
        q_out[pl.ds(c, probe, stride=cells), :] = blocks[c]
    r_out[...] = factors[:, :K]
    first_out[...] = factors[:, K:]


def shards(actions):
    _, probe, width, rows_y, depth = actions.shape
    devices = lax.axis_size("space")
    groups = K // probe
    slabs = devices // groups
    cells = width * rows_y
    chunk = cells // groups
    others = len(slab_offsets(slabs))
    scale = math.sqrt(width * rows_y * slabs * depth)
    dma = pltpu.SemaphoreType.DMA
    block = (groups, chunk, probe, depth)
    f32 = jnp.float32
    vmem = pl.BlockSpec(memory_space=pltpu.VMEM)
    q, factors = pl.pallas_call(
        functools.partial(kernel, slabs, groups, scale),
        out_shape=(
            jax.ShapeDtypeStruct(block, f32),
            jax.ShapeDtypeStruct((K, 2 * K), f32),
        ),
        in_specs=[pl.BlockSpec(memory_space=pltpu.HBM)],
        out_specs=(vmem, vmem),
        scratch_shapes=[
            pltpu.VMEM((probe * cells, depth), f32),
            pltpu.VMEM(block, f32),
            pltpu.VMEM((others,) + block, f32),
            pltpu.VMEM(block, f32),
            pltpu.VMEM((others,) + block, f32),
            pltpu.VMEM((2, K // 4, 128), f32),
            pltpu.VMEM((K // 4, 128), f32),
            pltpu.VMEM((2, K // 4, 128), f32),
            pltpu.VMEM((2, devices, K // 4, 128), f32),
            pltpu.VMEM((chunk, K, depth), f32),
            pltpu.VMEM((groups, chunk, K, depth), f32),
            pltpu.VMEM((K, 128), f32),
            pltpu.VMEM((K, 2 * chunk * depth), f32),
            dma((groups,)), dma((groups,)),
            dma((others, groups)), dma((others, groups)),
            dma(()), dma(()),
            dma((2, devices)), dma((2, devices)),
            dma((groups,)), dma((groups,)),
            dma(()),
        ],
        compiler_params=pltpu.CompilerParams(
            collective_id=0, has_side_effects=True, vmem_limit_bytes=20 * 1024 * 1024 + 16 * 4 * math.prod(block)
        ),
    )(actions.reshape(probe * cells, depth))
    q_fields, r, first = pl.pallas_call(
        finish,
        out_shape=(
            jax.ShapeDtypeStruct((probe * cells, depth), f32),
            jax.ShapeDtypeStruct((K, K), f32),
            jax.ShapeDtypeStruct((K, K), f32),
        ),
        in_specs=[vmem, vmem],
        out_specs=(vmem, vmem, vmem),
        compiler_params=pltpu.CompilerParams(vmem_limit_bytes=16 * 1024 * 1024),
    )(q.reshape(cells, probe, depth), factors)
    return (q_fields.reshape(1, probe, width, rows_y, depth), r, first)


def solution(mesh):
    in_specs = (P(("groups", "space"), None, None, None, None),)
    out_specs = (
        P(("groups", "space"), None, None, None, None),
        P("groups", None),
        P("groups", None),
    )
    return jax.shard_map(shards, mesh=mesh, in_specs=in_specs, out_specs=out_specs, check_vma=False)
```

```python
import functools
import math

import jax
import jax.numpy as jnp
from jax import lax
from jax.experimental import pallas as pl
from jax.experimental.pallas import tpu as pltpu
from jax.sharding import PartitionSpec as P

K = 64
YS = 2
highest = lax.Precision.HIGHEST
MESH = pl.DeviceIdType.MESH


def slab_offsets(slabs):
    return sorted({d % slabs for d in (1, -1, 2, -2)} - {0})


def walks(p, q, rows):
    gap = jnp.abs(p - q)
    low, high = jnp.minimum(p, q), jnp.maximum(p, q)
    at_start = jnp.where(low == 0, 1, 0)
    at_end = jnp.where(high == rows - 1, 1, 0)
    one = jnp.where(gap == 1, 1, 0)
    two = jnp.where(gap == 2, 1, 0) + jnp.where(gap == 0, 2 - at_start - at_end, 0)
    three = jnp.where(gap == 3, 1, 0) + jnp.where(gap == 1, 3 - at_start - at_end, 0)
    return one.astype(jnp.float32), two.astype(jnp.float32), three.astype(jnp.float32)


def eliminate(gram):
    lane = lax.broadcasted_iota(jnp.int32, (K, 128), 1)
    row_id = lax.broadcasted_iota(jnp.int32, (K, 128), 0)
    full = jnp.concatenate([gram, pltpu.roll(gram, K, 1)], axis=0)
    full = jnp.where(lane < K, full, jnp.where(lane - K == row_id, 1.0, 0.0))
    blocks = [full[8 * i : 8 * i + 8] for i in range(K // 8)]
    sub = lax.broadcasted_iota(jnp.int32, (8, 128), 0)
    count = len(blocks)
    shape = (8, 128)
    scaled = []
    for t in range(count):
        cols = [
            {i: jnp.broadcast_to(blocks[i][:, 8 * t + k : 8 * t + k + 1], shape) for i in range(t, count)}
            for k in range(8)
        ]
        pivots = jnp.ones(shape, jnp.float32)
        for r in range(8):
            pivot = jnp.broadcast_to(cols[r][t][r : r + 1], shape)
            pivots = jnp.where(sub == r, pivot, pivots)
            inverse = 1.0 / pivot
            factors = {i: cols[r][i] * inverse for i in range(t, count)}
            factors[t] = jnp.where(sub > r, factors[t], 0.0)
            for k in range(r + 1, 8):
                value = jnp.broadcast_to(cols[r][t][k : k + 1], shape)
                for i in range(t, count):
                    cols[k][i] = cols[k][i] - factors[i] * value
            row = jnp.broadcast_to(blocks[t][r : r + 1], shape)
            for i in range(t, count):
                blocks[i] = blocks[i] - factors[i] * row
        scaled.append(blocks[t] * lax.rsqrt(pivots))
    done = jnp.concatenate(scaled, axis=0)
    offset = jnp.where(lane < K, lane - row_id, row_id + K - lane)
    return jnp.where(offset >= 0, done, 0.0)


def kernel(
    slabs, groups, scale,
    source, q_out, factors_out,
    fields,
    own_send, cross_send, own_recv, cross_recv, part_send, part_recv, half_send, half_recv, mine, slab_rows, inverses, pair_rows,
    a_send, a_recv, c_send, c_recv, p_send, p_recv, h_send, h_recv, b_send, b_recv, in_sem,
):
    devices = slabs * groups
    me = lax.axis_index("space")
    slab, group = me // groups, lax.rem(me, groups)
    offsets = slab_offsets(slabs)
    probe = K // groups
    cells = fields.shape[0] // probe
    width = cells // YS
    chunk = cells // groups

    core = lax.rem(me, 2)
    load = pltpu.make_async_copy(source, fields, in_sem)
    load.start()
    barrier = pltpu.get_barrier_semaphore()
    for k in reversed(range(1, devices)):
        pl.semaphore_signal(barrier, inc=1, device_id={"space": lax.rem(me + k, devices)}, device_id_type=MESH)

    load.wait()
    field = jnp.stack([fields[pl.ds(c, probe, stride=cells), :] for c in range(cells)])
    field = field.reshape(width, YS, probe, 128)
    lane = lax.broadcasted_iota(jnp.int32, (probe, 128), 1)
    not_first, not_last = lane > 0, lane < 127

    def plane(u):
        flat = u.reshape(cells * probe, 128)
        low = pltpu.roll(flat, 1, 1).reshape(u.shape)
        high = pltpu.roll(flat, 127, 1).reshape(u.shape)
        total = jnp.where(not_first, low, 0.0) + jnp.where(not_last, high, 0.0)
        edge = jnp.zeros((1,) + u.shape[1:], u.dtype)
        return total + jnp.concatenate([u[1:], edge], 0) + jnp.concatenate([edge, u[:-1]], 0)

    d = 1.0 / 7.0
    one = plane(field)
    two = plane(one)
    three = plane(two)
    q0 = field * d + one * d**2 + two * d**3 + three * d**4
    q1 = field * d**2 + one * (2 * d**3) + two * (3 * d**4)
    q2 = field * d**3 + one * (3 * d**4)
    q3 = field * d**4

    def spread(other, own):
        rows = []
        for b in range(YS):
            a = 1 - b
            _, w2, _ = walks(YS * slab + b, YS * other + b, YS * slabs)
            w1, _, w3 = walks(YS * slab + a, YS * other + b, YS * slabs)
            value = w2 * q2[:, b] + w1 * q1[:, a] + w3 * q3[:, a]
            rows.append(q0[:, b] + value if own else value)
        return jnp.stack(rows, axis=1).reshape(groups, chunk, probe, 128)

    for n, offset in enumerate(offsets):
        cross_send[n] = spread(lax.rem(slab + offset, slabs), False)

    pl.semaphore_wait(barrier, devices - 1)

    started = []

    def send(src, dst, send_sem, recv_sem, peer):
        copy = pltpu.make_async_remote_copy(
            src_ref=src, dst_ref=dst, send_sem=send_sem, recv_sem=recv_sem,
            device_id={"space": peer}, device_id_type=MESH,
        )
        copy.start()
        started.append(copy)

    def drain(limit):
        while len(started) > limit:
            started.pop(0).wait_send()

    def arrive(dst, sem):
        pltpu.make_async_copy(dst, dst, sem).wait()

    for n, offset in enumerate(offsets):
        there = lax.rem(slab + offset, slabs)
        for k in range(groups):
            g = lax.rem(group + k, groups)
            send(cross_send.at[n, g], cross_recv.at[n, group], c_send.at[n, g], c_recv.at[n, group], there * groups + g)
    own_send[...] = spread(slab, True)
    for k in range(1, groups):
        g = lax.rem(group + k, groups)
        send(own_send.at[g], own_recv.at[group], a_send.at[g], a_recv.at[group], slab * groups + g)
    own_recv[group] = own_send[group]
    for k in range(1, groups):
        g = lax.rem(group + k, groups)
        arrive(own_recv.at[g], a_recv.at[g])
    for n in range(len(offsets)):
        for g in range(groups):
            arrive(cross_recv.at[n, g], c_recv.at[n, g])
    total = own_recv[...]
    for n in range(len(offsets)):
        total = total + cross_recv[n]
    for c in range(chunk):
        mine[c] = total[:, c].reshape(K, 128)
    matrix = jnp.concatenate([mine[c] for c in range(chunk)], axis=1)

    beside_me = 1 - 2 * core

    def share():
        for k in reversed(range(2, groups, 2)):
            g = lax.rem(group + k, groups)
            send(mine, slab_rows.at[group], b_send.at[g], b_recv.at[group], slab * groups + g)
        g = group + beside_me
        send(mine, slab_rows.at[group], b_send.at[g], b_recv.at[group], slab * groups + g)
        slab_rows[group] = mine[...]

    def relay():
        for k in range(2, groups, 2):
            g = lax.rem(group + k, groups)
            arrive(slab_rows.at[g], b_recv.at[g])
            send(slab_rows.at[g], slab_rows.at[g], b_send.at[g + beside_me], b_recv.at[g], me + beside_me)

    def summed(rows):
        before = len(started)
        part = lax.dot_general(
            rows, rows, (((1,), (1,)), ((), ())), precision=highest, preferred_element_type=jnp.float32
        )
        part = jnp.concatenate([part[: K // 2], part[K // 2 :]], axis=1)
        part_send[...] = part.reshape(2, K // 4, 128)
        send(part_send.at[1 - core], part_recv, p_send, p_recv, me + beside_me)
        arrive(part_recv, p_recv)
        return added(part_send[core] + part_recv[...], 0, share, before)

    def added(half, turn, beside, before):
        half_send[turn] = half
        for k in reversed(range(1, devices)):
            peer = lax.rem(me + k, devices)
            send(half_send.at[turn], half_recv.at[turn, me], h_send.at[turn, peer], h_recv.at[turn, me], peer)
        half_recv[turn, me] = half_send[turn]
        beside()
        drain(len(started) - before)
        for k in range(1, devices):
            peer = lax.rem(me + k, devices)
            arrive(half_recv.at[turn, peer], h_recv.at[turn, peer])
        return jnp.sum(half_recv[turn].reshape(devices // 2, K // 2, 128), axis=0)

    both_one = eliminate(summed(matrix))
    beside = group + beside_me
    arrive(slab_rows.at[beside], b_recv.at[beside])
    pair = jnp.concatenate([matrix] + [slab_rows[beside, c] for c in range(chunk)], axis=1)
    basis_one = jnp.dot(both_one[:, K:], pair, precision=highest, preferred_element_type=jnp.float32)
    pair_rows[...] = basis_one
    quarter = K // 4
    low = pl.multiple_of(core * quarter, quarter)
    mine_low, mine_high = pair_rows[pl.ds(low, quarter), :], pair_rows[pl.ds(low + K // 2, quarter), :]
    part = lax.dot_general(
        jnp.concatenate([mine_low, mine_high], axis=0), basis_one, (((1,), (1,)), ((), ())),
        precision=highest, preferred_element_type=jnp.float32,
    )
    part = jnp.concatenate([part[:quarter], part[quarter:]], axis=1)
    both_two = eliminate(added(part, 1, relay, len(started)))
    product = jnp.dot(both_two[:, K:] * scale, both_one[:, K:], precision=highest, preferred_element_type=jnp.float32)
    inverses[:, :K] = product
    weights = inverses[pl.ds(pl.multiple_of(group * probe, probe), probe), :][:, :K]
    for k in range(2, groups, 2):
        g = lax.rem(group + k, groups) + beside_me
        arrive(slab_rows.at[g], b_recv.at[g])
    for g in range(groups):
        rows = jnp.concatenate([slab_rows[g, c] for c in range(chunk)], axis=1)
        basis = jnp.dot(weights, rows, precision=highest, preferred_element_type=jnp.float32)
        for c in range(chunk):
            q_out[g, c] = basis[:, 128 * c : 128 * c + 128]
    first = both_one[:, :K]
    r = jnp.dot(both_two[:, :K], first, precision=highest, preferred_element_type=jnp.float32)
    factors_out[...] = jnp.concatenate([r, first], axis=1) * (1.0 / scale)
    drain(0)


def finish(blocks, factors, q_out, r_out, first_out):
    cells, probe, _ = blocks.shape
    for c in range(cells):
        q_out[pl.ds(c, probe, stride=cells), :] = blocks[c]
    r_out[...] = factors[:, :K]
    first_out[...] = factors[:, K:]


def shards(actions):
    _, probe, width, rows_y, depth = actions.shape
    devices = lax.axis_size("space")
    groups = K // probe
    slabs = devices // groups
    cells = width * rows_y
    chunk = cells // groups
    others = len(slab_offsets(slabs))
    scale = math.sqrt(width * rows_y * slabs * depth)
    dma = pltpu.SemaphoreType.DMA
    block = (groups, chunk, probe, depth)
    f32 = jnp.float32
    vmem = pl.BlockSpec(memory_space=pltpu.VMEM)
    q, factors = pl.pallas_call(
        functools.partial(kernel, slabs, groups, scale),
        out_shape=(
            jax.ShapeDtypeStruct(block, f32),
            jax.ShapeDtypeStruct((K, 2 * K), f32),
        ),
        in_specs=[pl.BlockSpec(memory_space=pltpu.HBM)],
        out_specs=(vmem, vmem),
        scratch_shapes=[
            pltpu.VMEM((probe * cells, depth), f32),
            pltpu.VMEM(block, f32),
            pltpu.VMEM((others,) + block, f32),
            pltpu.VMEM(block, f32),
            pltpu.VMEM((others,) + block, f32),
            pltpu.VMEM((2, K // 4, 128), f32),
            pltpu.VMEM((K // 4, 128), f32),
            pltpu.VMEM((2, K // 4, 128), f32),
            pltpu.VMEM((2, devices, K // 4, 128), f32),
            pltpu.VMEM((chunk, K, depth), f32),
            pltpu.VMEM((groups, chunk, K, depth), f32),
            pltpu.VMEM((K, 128), f32),
            pltpu.VMEM((K, 2 * chunk * depth), f32),
            dma((groups,)), dma((groups,)),
            dma((others, groups)), dma((others, groups)),
            dma(()), dma(()),
            dma((2, devices)), dma((2, devices)),
            dma((groups,)), dma((groups,)),
            dma(()),
        ],
        compiler_params=pltpu.CompilerParams(
            collective_id=0, has_side_effects=True, vmem_limit_bytes=20 * 1024 * 1024 + 16 * 4 * math.prod(block)
        ),
    )(pltpu.with_memory_space_constraint(actions.reshape(probe * cells, depth), pltpu.HBM))
    q_fields, r, first = pl.pallas_call(
        finish,
        out_shape=(
            jax.ShapeDtypeStruct((probe * cells, depth), f32),
            jax.ShapeDtypeStruct((K, K), f32),
            jax.ShapeDtypeStruct((K, K), f32),
        ),
        in_specs=[vmem, vmem],
        out_specs=(vmem, vmem, vmem),
        compiler_params=pltpu.CompilerParams(vmem_limit_bytes=16 * 1024 * 1024),
    )(q.reshape(cells, probe, depth), factors)
    return (q_fields.reshape(1, probe, width, rows_y, depth), r, first)


def solution(mesh):
    in_specs = (P(("groups", "space"), None, None, None, None),)
    out_specs = (
        P(("groups", "space"), None, None, None, None),
        P("groups", None),
        P("groups", None),
    )
    return jax.shard_map(shards, mesh=mesh, in_specs=in_specs, out_specs=out_specs, check_vma=False)
```

```python
import functools
import math

import jax
import jax.numpy as jnp
from jax import lax
from jax.experimental import pallas as pl
from jax.experimental.pallas import tpu as pltpu
from jax.sharding import PartitionSpec as P

K = 64
YS = 2
highest = lax.Precision.HIGHEST
MESH = pl.DeviceIdType.MESH


def slab_offsets(slabs):
    return sorted({d % slabs for d in (1, -1, 2, -2)} - {0})


def walks(p, q, rows):
    gap = jnp.abs(p - q)
    low, high = jnp.minimum(p, q), jnp.maximum(p, q)
    at_start = jnp.where(low == 0, 1, 0)
    at_end = jnp.where(high == rows - 1, 1, 0)
    one = jnp.where(gap == 1, 1, 0)
    two = jnp.where(gap == 2, 1, 0) + jnp.where(gap == 0, 2 - at_start - at_end, 0)
    three = jnp.where(gap == 3, 1, 0) + jnp.where(gap == 1, 3 - at_start - at_end, 0)
    return one.astype(jnp.float32), two.astype(jnp.float32), three.astype(jnp.float32)


def eliminate(gram):
    lane = lax.broadcasted_iota(jnp.int32, (K, 128), 1)
    row_id = lax.broadcasted_iota(jnp.int32, (K, 128), 0)
    full = jnp.concatenate([gram, pltpu.roll(gram, K, 1)], axis=0)
    full = jnp.where(lane < K, full, jnp.where(lane - K == row_id, 1.0, 0.0))
    blocks = [full[8 * i : 8 * i + 8] for i in range(K // 8)]
    sub = lax.broadcasted_iota(jnp.int32, (8, 128), 0)
    count = len(blocks)
    shape = (8, 128)
    scaled = []
    for t in range(count):
        cols = [
            {i: jnp.broadcast_to(blocks[i][:, 8 * t + k : 8 * t + k + 1], shape) for i in range(t, count)}
            for k in range(8)
        ]
        pivots = jnp.ones(shape, jnp.float32)
        for r in range(8):
            pivot = jnp.broadcast_to(cols[r][t][r : r + 1], shape)
            pivots = jnp.where(sub == r, pivot, pivots)
            inverse = 1.0 / pivot
            factors = {i: cols[r][i] * inverse for i in range(t, count)}
            factors[t] = jnp.where(sub > r, factors[t], 0.0)
            for k in range(r + 1, 8):
                value = jnp.broadcast_to(cols[r][t][k : k + 1], shape)
                for i in range(t, count):
                    cols[k][i] = cols[k][i] - factors[i] * value
            row = jnp.broadcast_to(blocks[t][r : r + 1], shape)
            for i in range(t, count):
                blocks[i] = blocks[i] - factors[i] * row
        scaled.append(blocks[t] * lax.rsqrt(pivots))
    done = jnp.concatenate(scaled, axis=0)
    offset = jnp.where(lane < K, lane - row_id, row_id + K - lane)
    return jnp.where(offset >= 0, done, 0.0)


def kernel(
    slabs, groups, scale,
    source, q_out, factors_out,
    fields,
    own_send, cross_send, own_recv, cross_recv, part_send, part_recv, half_send, half_recv, mine, slab_rows, inverses, pair_rows,
    a_send, a_recv, c_send, c_recv, p_send, p_recv, h_send, h_recv, b_send, b_recv, in_sem,
):
    devices = slabs * groups
    me = lax.axis_index("space")
    slab, group = me // groups, lax.rem(me, groups)
    offsets = slab_offsets(slabs)
    probe = K // groups
    cells = fields.shape[0] // probe
    width = cells // YS
    chunk = cells // groups

    core = lax.rem(me, 2)
    load = pltpu.make_async_copy(source, fields, in_sem)
    load.start()
    barrier = pltpu.get_barrier_semaphore()
    for k in reversed(range(1, devices)):
        pl.semaphore_signal(barrier, inc=1, device_id={"space": lax.rem(me + k, devices)}, device_id_type=MESH)

    load.wait()
    field = jnp.stack([fields[pl.ds(c, probe, stride=cells), :] for c in range(cells)])
    field = field.reshape(width, YS, probe, 128)
    lane = lax.broadcasted_iota(jnp.int32, (probe, 128), 1)
    not_first, not_last = lane > 0, lane < 127

    def plane(u):
        flat = u.reshape(cells * probe, 128)
        low = pltpu.roll(flat, 1, 1).reshape(u.shape)
        high = pltpu.roll(flat, 127, 1).reshape(u.shape)
        total = jnp.where(not_first, low, 0.0) + jnp.where(not_last, high, 0.0)
        edge = jnp.zeros((1,) + u.shape[1:], u.dtype)
        return total + jnp.concatenate([u[1:], edge], 0) + jnp.concatenate([edge, u[:-1]], 0)

    d = 1.0 / 7.0
    one = plane(field)
    two = plane(one)
    three = plane(two)
    q0 = field * d + one * d**2 + two * d**3 + three * d**4
    q1 = field * d**2 + one * (2 * d**3) + two * (3 * d**4)
    q2 = field * d**3 + one * (3 * d**4)
    q3 = field * d**4

    def spread(other, own):
        rows = []
        for b in range(YS):
            a = 1 - b
            _, w2, _ = walks(YS * slab + b, YS * other + b, YS * slabs)
            w1, _, w3 = walks(YS * slab + a, YS * other + b, YS * slabs)
            value = w2 * q2[:, b] + w1 * q1[:, a] + w3 * q3[:, a]
            rows.append(q0[:, b] + value if own else value)
        return jnp.stack(rows, axis=1).reshape(groups, chunk, probe, 128)

    for n, offset in enumerate(offsets):
        cross_send[n] = spread(lax.rem(slab + offset, slabs), False)

    own_send[...] = spread(slab, True)
    pl.semaphore_wait(barrier, devices - 1)

    started = []

    def send(src, dst, send_sem, recv_sem, peer):
        copy = pltpu.make_async_remote_copy(
            src_ref=src, dst_ref=dst, send_sem=send_sem, recv_sem=recv_sem,
            device_id={"space": peer}, device_id_type=MESH,
        )
        copy.start()
        started.append(copy)

    def drain(limit):
        while len(started) > limit:
            started.pop(0).wait_send()

    def arrive(dst, sem):
        pltpu.make_async_copy(dst, dst, sem).wait()

    for n, offset in enumerate(offsets):
        there = lax.rem(slab + offset, slabs)
        for k in range(groups):
            g = lax.rem(group + k, groups)
            send(cross_send.at[n, g], cross_recv.at[n, group], c_send.at[n, g], c_recv.at[n, group], there * groups + g)
    for k in range(1, groups):
        g = lax.rem(group + k, groups)
        send(own_send.at[g], own_recv.at[group], a_send.at[g], a_recv.at[group], slab * groups + g)
    own_recv[group] = own_send[group]
    for k in range(1, groups):
        g = lax.rem(group + k, groups)
        arrive(own_recv.at[g], a_recv.at[g])
    for n in range(len(offsets)):
        for g in range(groups):
            arrive(cross_recv.at[n, g], c_recv.at[n, g])
    total = own_recv[...]
    for n in range(len(offsets)):
        total = total + cross_recv[n]
    for c in range(chunk):
        mine[c] = total[:, c].reshape(K, 128)
    matrix = jnp.concatenate([mine[c] for c in range(chunk)], axis=1)

    beside_me = 1 - 2 * core

    def share():
        for k in reversed(range(2, groups, 2)):
            g = lax.rem(group + k, groups)
            send(mine, slab_rows.at[group], b_send.at[g], b_recv.at[group], slab * groups + g)
        g = group + beside_me
        send(mine, slab_rows.at[group], b_send.at[g], b_recv.at[group], slab * groups + g)
        slab_rows[group] = mine[...]

    def relay():
        for k in range(2, groups, 2):
            g = lax.rem(group + k, groups)
            arrive(slab_rows.at[g], b_recv.at[g])
            send(slab_rows.at[g], slab_rows.at[g], b_send.at[g + beside_me], b_recv.at[g], me + beside_me)

    def summed(rows):
        before = len(started)
        part = lax.dot_general(
            rows, rows, (((1,), (1,)), ((), ())), precision=highest, preferred_element_type=jnp.float32
        )
        part = jnp.concatenate([part[: K // 2], part[K // 2 :]], axis=1)
        part_send[...] = part.reshape(2, K // 4, 128)
        send(part_send.at[1 - core], part_recv, p_send, p_recv, me + beside_me)
        arrive(part_recv, p_recv)
        return added(part_send[core] + part_recv[...], 0, share, before)

    def added(half, turn, beside, before):
        half_send[turn] = half
        for k in reversed(range(1, devices)):
            peer = lax.rem(me + k, devices)
            send(half_send.at[turn], half_recv.at[turn, me], h_send.at[turn, peer], h_recv.at[turn, me], peer)
        half_recv[turn, me] = half_send[turn]
        beside()
        drain(len(started) - before)
        for k in range(1, devices):
            peer = lax.rem(me + k, devices)
            arrive(half_recv.at[turn, peer], h_recv.at[turn, peer])
        return jnp.sum(half_recv[turn].reshape(devices // 2, K // 2, 128), axis=0)

    both_one = eliminate(summed(matrix))
    beside = group + beside_me
    arrive(slab_rows.at[beside], b_recv.at[beside])
    pair = jnp.concatenate([matrix] + [slab_rows[beside, c] for c in range(chunk)], axis=1)
    basis_one = jnp.dot(both_one[:, K:], pair, precision=highest, preferred_element_type=jnp.float32)
    pair_rows[...] = basis_one
    quarter = K // 4
    low = pl.multiple_of(core * quarter, quarter)
    mine_low, mine_high = pair_rows[pl.ds(low, quarter), :], pair_rows[pl.ds(low + K // 2, quarter), :]
    part = lax.dot_general(
        jnp.concatenate([mine_low, mine_high], axis=0), basis_one, (((1,), (1,)), ((), ())),
        precision=highest, preferred_element_type=jnp.float32,
    )
    part = jnp.concatenate([part[:quarter], part[quarter:]], axis=1)
    both_two = eliminate(added(part, 1, relay, len(started)))
    product = jnp.dot(both_two[:, K:] * scale, both_one[:, K:], precision=highest, preferred_element_type=jnp.float32)
    inverses[:, :K] = product
    weights = inverses[pl.ds(pl.multiple_of(group * probe, probe), probe), :][:, :K]
    for k in range(2, groups, 2):
        g = lax.rem(group + k, groups) + beside_me
        arrive(slab_rows.at[g], b_recv.at[g])
    for g in range(groups):
        rows = jnp.concatenate([slab_rows[g, c] for c in range(chunk)], axis=1)
        basis = jnp.dot(weights, rows, precision=highest, preferred_element_type=jnp.float32)
        for c in range(chunk):
            q_out[g, c] = basis[:, 128 * c : 128 * c + 128]
    first = both_one[:, :K]
    r = jnp.dot(both_two[:, :K], first, precision=highest, preferred_element_type=jnp.float32)
    factors_out[...] = jnp.concatenate([r, first], axis=1) * (1.0 / scale)
    drain(0)


def finish(blocks, factors, q_out, r_out, first_out):
    cells, probe, _ = blocks.shape
    for c in range(cells):
        q_out[pl.ds(c, probe, stride=cells), :] = blocks[c]
    r_out[...] = factors[:, :K]
    first_out[...] = factors[:, K:]


def shards(actions):
    _, probe, width, rows_y, depth = actions.shape
    devices = lax.axis_size("space")
    groups = K // probe
    slabs = devices // groups
    cells = width * rows_y
    chunk = cells // groups
    others = len(slab_offsets(slabs))
    scale = math.sqrt(width * rows_y * slabs * depth)
    dma = pltpu.SemaphoreType.DMA
    block = (groups, chunk, probe, depth)
    f32 = jnp.float32
    vmem = pl.BlockSpec(memory_space=pltpu.VMEM)
    q, factors = pl.pallas_call(
        functools.partial(kernel, slabs, groups, scale),
        out_shape=(
            jax.ShapeDtypeStruct(block, f32),
            jax.ShapeDtypeStruct((K, 2 * K), f32),
        ),
        in_specs=[pl.BlockSpec(memory_space=pltpu.HBM)],
        out_specs=(vmem, vmem),
        scratch_shapes=[
            pltpu.VMEM((probe * cells, depth), f32),
            pltpu.VMEM(block, f32),
            pltpu.VMEM((others,) + block, f32),
            pltpu.VMEM(block, f32),
            pltpu.VMEM((others,) + block, f32),
            pltpu.VMEM((2, K // 4, 128), f32),
            pltpu.VMEM((K // 4, 128), f32),
            pltpu.VMEM((2, K // 4, 128), f32),
            pltpu.VMEM((2, devices, K // 4, 128), f32),
            pltpu.VMEM((chunk, K, depth), f32),
            pltpu.VMEM((groups, chunk, K, depth), f32),
            pltpu.VMEM((K, 128), f32),
            pltpu.VMEM((K, 2 * chunk * depth), f32),
            dma((groups,)), dma((groups,)),
            dma((others, groups)), dma((others, groups)),
            dma(()), dma(()),
            dma((2, devices)), dma((2, devices)),
            dma((groups,)), dma((groups,)),
            dma(()),
        ],
        compiler_params=pltpu.CompilerParams(
            collective_id=0, has_side_effects=True, vmem_limit_bytes=20 * 1024 * 1024 + 16 * 4 * math.prod(block)
        ),
    )(pltpu.with_memory_space_constraint(actions.reshape(probe * cells, depth), pltpu.HBM))
    q_fields, r, first = pl.pallas_call(
        finish,
        out_shape=(
            jax.ShapeDtypeStruct((probe * cells, depth), f32),
            jax.ShapeDtypeStruct((K, K), f32),
            jax.ShapeDtypeStruct((K, K), f32),
        ),
        in_specs=[vmem, vmem],
        out_specs=(vmem, vmem, vmem),
        compiler_params=pltpu.CompilerParams(vmem_limit_bytes=16 * 1024 * 1024),
    )(q.reshape(cells, probe, depth), factors)
    return (q_fields.reshape(1, probe, width, rows_y, depth), r, first)


def solution(mesh):
    in_specs = (P(("groups", "space"), None, None, None, None),)
    out_specs = (
        P(("groups", "space"), None, None, None, None),
        P("groups", None),
        P("groups", None),
    )
    return jax.shard_map(shards, mesh=mesh, in_specs=in_specs, out_specs=out_specs, check_vma=False)
```
